32 devices in a mesh: grp: 2 (over x), gx: 8 (over z, y), gy: 2 (over core).
Axes of the slice: x: 2, y: 2, z: 4, core: 2. Of those that a mesh axis runs over, the one named last changes fastest.
Arguments:
- loaded_fields: bfloat16 [2, 32, 16, 128], P(None, ('grp', 'gx'), 'gy'), parts along dimension 1, may hold values from -6 to 6
- brick_home: int32 [16], P('grp'), parts along dimension 0, may hold values from 0 to 7, each once
- liquid_mask: int32 [32, 16, 128], P(('grp', 'gx'), 'gy'), parts along dimension 0, may hold values 0 or 1
- density_class: int32 [32, 16, 128], P(('grp', 'gx'), 'gy'), parts along dimension 0, may hold values from 0 to 3
- inverse_density: float32 [4], replicated, may hold values from 0.25 to 4
- conv_a: bfloat16 [27, 64, 3], replicated, may hold values from -0.625 to 0.625
- bias_a: float32 [64], replicated, may hold values from -3 to 3
- conv_b: bfloat16 [27, 64, 64], replicated, may hold values from -0.15625 to 0.15625
- bias_b: float32 [64], replicated, may hold values from -3 to 3
- conv_c: bfloat16 [27, 64, 64], replicated, may hold values from -0.15625 to 0.15625
- bias_c: float32 [64], replicated, may hold values from -3 to 3
- head_weight: bfloat16 [64], replicated, may hold values from -0.75 to 0.75
- head_bias: float32 [1], replicated, may hold values from -3 to 3
Outputs:
- pressure: float32 [32, 16, 128], P(('grp', 'gx'), 'gy'), parts along dimension 0
- loss: float32 [2], P('grp'), parts along dimension 0
- grad_conv_a: float32 [54, 64, 3], P('grp'), parts along dimension 0
- grad_bias_a: float32 [128], P('grp'), parts along dimension 0
- grad_conv_b: float32 [54, 64, 64], P('grp'), parts along dimension 0
- grad_bias_b: float32 [128], P('grp'), parts along dimension 0
- grad_conv_c: float32 [54, 64, 64], P('grp'), parts along dimension 0
- grad_bias_c: float32 [128], P('grp'), parts along dimension 0
- grad_head_weight: float32 [128], P('grp'), parts along dimension 0
The draws below stay inside these ranges and needn't reach their ends.
There are 2 independent parts, one for each index of `grp`. The reference program is written for one: setup_inputs(seed, part) draws one part's arguments, and reference() takes and returns one part's arrays. A program takes and returns all parts, laid end to end along the dimension named above; an argument that names none is the same for every part. Nothing has to cross between parts.
Inputs may be any that keep to these rules, and one draw needn't show every extreme that they name: `brick_home`: a permutation of 0 to 7.
All inputs are finite; a program needn't handle non-finite values. No bound on the sum of `liquid_mask` on one device may be relied on, other than what follows from the above.
Results may differ from the reference program's by a relative error of at most 0.0041.
The reference program's roundings to bfloat16 on the way count: a program that leaves them out, or rounds other values in their place, can miss the bound.
Values may be sent and summed in bfloat16 or wider, within the bound.
A program may use at most 64 MiB of HBM per device.

```python
import math
import jax
import jax.numpy as jnp
from jax import lax

HID = 64
CIN = 3
NCLASS = 4
CX = 2
NZ = 128
NX = 16
NY = 16
N_GX = 8


def place_ends(entries, key, least, largest):
    spot = [jax.random.randint(jax.random.fold_in(key, axis), (), 0, length) for axis, length in enumerate(entries.shape)]
    main_axis = entries.shape.index(max(entries.shape))
    beside = spot[:main_axis] + [(spot[main_axis] + 1) % entries.shape[main_axis]] + spot[main_axis + 1:]
    return entries.at[tuple(spot)].set(least).at[tuple(beside)].set(largest)


def levels(key, shape, cuts, least, largest):
    def one(axis_at, parts):
        draws = jax.random.uniform(jax.random.fold_in(jax.random.fold_in(key, 6), axis_at), (parts,), jnp.float32, least / len(cuts), largest / len(cuts))
        return jnp.repeat(jnp.exp(draws), shape[axis_at] // parts).reshape((-1,) + (1,) * (len(shape) - axis_at - 1))

    gain = one(*cuts[0])
    for cut in cuts[1:]:
        gain = gain * one(*cut)
    return gain


def bell_draw(own_key, extent, deviation, reach, cuts=(), kind=jnp.bfloat16):
    level = levels(own_key, extent, cuts, -0.22, 0.18) if cuts else 1.0
    drawn = jax.random.normal(own_key, extent, jnp.float32) * deviation * level
    return jnp.minimum(jnp.maximum(drawn, -reach), reach).astype(kind)


def setup_inputs(seed: int = 0, part: int = 0) -> dict:
    key_of = jax.random.split(jax.random.key(seed), 14)
    own_keys = jax.random.split(jax.random.fold_in(key_of[13], part), 14)
    loaded_fields = bell_draw(own_keys[0], (2, NX, NY, NZ), 1.0, 6.0, ((1, 8), (2, 2)))
    brick_home = jax.random.permutation(own_keys[1], N_GX).astype(jnp.int32)
    liquid_mask = place_ends((jax.random.randint(own_keys[2], (NX, NY, NZ), 0, 4) < 3).astype(jnp.int32), jax.random.fold_in(own_keys[2], 1), 0, 1)
    density_class = place_ends(jax.random.randint(own_keys[3], (NX, NY, NZ), 0, NCLASS), jax.random.fold_in(own_keys[3], 1), 0, NCLASS - 1).astype(jnp.int32)
    inverse_density = jnp.clip(jnp.exp(jax.random.uniform(key_of[4], (NCLASS,), jnp.float32, math.log(0.25), math.log(4.0))), 0.25, 4.0)
    conv_a = bell_draw(key_of[5], (27, HID, CIN), (27 * CIN) ** -0.5, 0.625)
    bias_a = bell_draw(key_of[6], (HID,), 0.5, 3.0, (), jnp.float32)
    conv_b = bell_draw(key_of[7], (27, HID, HID), (27 * HID) ** -0.5, 0.15625)
    bias_b = bell_draw(key_of[8], (HID,), 0.5, 3.0, (), jnp.float32)
    conv_c = bell_draw(key_of[9], (27, HID, HID), (27 * HID) ** -0.5, 0.15625)
    bias_c = bell_draw(key_of[10], (HID,), 0.5, 3.0, (), jnp.float32)
    head_weight = bell_draw(key_of[11], (HID,), HID ** -0.5, 0.75)
    head_bias = bell_draw(key_of[12], (1,), 0.5, 3.0, (), jnp.float32)
    return {"loaded_fields": loaded_fields, "brick_home": brick_home, "liquid_mask": liquid_mask, "density_class": density_class, "inverse_density": inverse_density, "conv_a": conv_a, "bias_a": bias_a, "conv_b": conv_b, "bias_b": bias_b, "conv_c": conv_c, "bias_c": bias_c, "head_weight": head_weight, "head_bias": head_bias}


PRECISE = lax.Precision.HIGHEST
TAP_LIST = [(first, second, third) for first in range(3) for second in range(3) for third in range(3)]
NEIGHBOUR_LIST = [(2, 1, 1), (0, 1, 1), (1, 2, 1), (1, 0, 1), (1, 1, 2), (1, 1, 0)]

def pad_space(values):
    widths = [(0, 0)] * (values.ndim - 3) + [(1, 1)] * 3
    return jnp.pad(values, widths)

def conv_forward(inputs, weights):
    padded = pad_space(inputs)
    size_x, size_y, size_z = inputs.shape[1:]
    total = jnp.zeros((weights.shape[1], size_x, size_y, size_z), inputs.dtype)
    for tap_index, (first, second, third) in enumerate(TAP_LIST):
        window = padded[:, first:first + size_x, second:second + size_y, third:third + size_z]
        total = total + jnp.einsum('oi,ixyz->oxyz', weights[tap_index], window, precision=PRECISE)
    return total

def conv_weight_grad(inputs, grads):
    padded = pad_space(inputs)
    size_x, size_y, size_z = inputs.shape[1:]
    parts_list = []
    for first, second, third in TAP_LIST:
        window = padded[:, first:first + size_x, second:second + size_y, third:third + size_z]
        parts_list.append(jnp.einsum('oxyz,ixyz->oi', grads, window, precision=PRECISE))
    return jnp.stack(parts_list)

def conv_input_grad(grads, weights):
    padded = pad_space(grads)
    size_x, size_y, size_z = grads.shape[1:]
    total = jnp.zeros((weights.shape[2], size_x, size_y, size_z), grads.dtype)
    for tap_index, (first, second, third) in enumerate(TAP_LIST):
        window = padded[:, 2 - first:2 - first + size_x, 2 - second:2 - second + size_y, 2 - third:2 - third + size_z]
        total = total + jnp.einsum('oi,oxyz->ixyz', weights[tap_index], window, precision=PRECISE)
    return total

def silu_slope(values):
    sigma = jax.nn.sigmoid(values)
    return sigma * (1.0 + values * (1.0 - sigma))

def face_coefs(scaled, liquid):
    padded_scaled = pad_space(scaled)
    padded_liquid = pad_space(liquid)
    size_x, size_y, size_z = scaled.shape
    result = []
    for first, second, third in NEIGHBOUR_LIST:
        near_scaled = padded_scaled[first:first + size_x, second:second + size_y, third:third + size_z]
        near_liquid = padded_liquid[first:first + size_x, second:second + size_y, third:third + size_z]
        result.append(0.5 * (scaled * near_liquid + near_scaled * liquid))
    return result

def apply_operator(values, coefs):
    padded = pad_space(values)
    size_x, size_y, size_z = values.shape
    total = jnp.zeros_like(values)
    for coef, (first, second, third) in zip(coefs, NEIGHBOUR_LIST):
        near = padded[first:first + size_x, second:second + size_y, third:third + size_z]
        total = total + coef * (near - values)
    return total

def reference(loaded_fields, brick_home, liquid_mask, density_class, inverse_density, conv_a, bias_a, conv_b, bias_b, conv_c, bias_c, head_weight, head_bias):
    slots = jnp.arange(N_GX, dtype=jnp.int32)
    inverse = lax.optimization_barrier(jnp.sum(jnp.where(brick_home[None, :] == slots[:, None], slots[None, :], 0), axis=1)).astype(jnp.int32)
    fields = loaded_fields.reshape(2, N_GX, CX, NY, NZ)[:, inverse].reshape(2, NX, NY, NZ)
    liquid = liquid_mask.astype(jnp.float32)
    classes = jnp.arange(NCLASS, dtype=jnp.int32)
    scale = lax.optimization_barrier(jnp.sum(jnp.where(density_class[None] == classes[:, None, None, None], inverse_density[:, None, None, None], 0.0), axis=0))
    inputs = jnp.concatenate([fields, liquid.astype(jnp.bfloat16)[None]], axis=0)
    pre_one = conv_forward(inputs.astype(jnp.float32), conv_a.astype(jnp.float32)) + bias_a[:, None, None, None]
    act_one = (jax.nn.silu(pre_one) * liquid).astype(jnp.bfloat16)
    pre_two = conv_forward(act_one.astype(jnp.float32), conv_b.astype(jnp.float32)) + bias_b[:, None, None, None]
    act_two = (jax.nn.silu(pre_two) * liquid).astype(jnp.bfloat16)
    pre_three = conv_forward(act_two.astype(jnp.float32), conv_c.astype(jnp.float32)) + bias_c[:, None, None, None]
    act_three = (jax.nn.silu(pre_three) * liquid).astype(jnp.bfloat16)
    head_float = head_weight.astype(jnp.float32)
    pressure = liquid * (jnp.einsum('o,oxyz->xyz', head_float, act_three.astype(jnp.float32), precision=PRECISE) + head_bias[0])
    coefs = face_coefs(scale * liquid, liquid)
    residual = apply_operator(pressure, coefs) - liquid * fields[1].astype(jnp.float32)
    cells = NX * NY * NZ
    loss = jnp.sum(residual * residual) / cells
    grad_score = liquid * apply_operator(2.0 * residual / cells, coefs)
    grad_head_weight = jnp.einsum('xyz,oxyz->o', grad_score, act_three.astype(jnp.float32), precision=PRECISE)
    grad_three = (grad_score[None] * head_float[:, None, None, None] * liquid * silu_slope(pre_three)).astype(jnp.bfloat16)
    grad_three_f = grad_three.astype(jnp.float32)
    grad_conv_c = conv_weight_grad(act_two.astype(jnp.float32), grad_three_f)
    grad_bias_c = lax.optimization_barrier(jnp.sum(grad_three_f, axis=(1, 2, 3)))
    back_two = conv_input_grad(grad_three_f, conv_c.astype(jnp.float32))
    grad_two = (back_two * liquid * silu_slope(pre_two)).astype(jnp.bfloat16)
    grad_two_f = grad_two.astype(jnp.float32)
    grad_conv_b = conv_weight_grad(act_one.astype(jnp.float32), grad_two_f)
    grad_bias_b = lax.optimization_barrier(jnp.sum(grad_two_f, axis=(1, 2, 3)))
    back_one = conv_input_grad(grad_two_f, conv_b.astype(jnp.float32))
    grad_one = (back_one * liquid * silu_slope(pre_one)).astype(jnp.bfloat16)
    grad_one_f = grad_one.astype(jnp.float32)
    grad_conv_a = conv_weight_grad(inputs.astype(jnp.float32), grad_one_f)
    grad_bias_a = lax.optimization_barrier(jnp.sum(grad_one_f, axis=(1, 2, 3)))
    return (pressure, loss.reshape(1), grad_conv_a, grad_bias_a, grad_conv_b, grad_bias_b, grad_conv_c, grad_bias_c, grad_head_weight)
```

```python
import functools

import jax
import jax.numpy as jnp
from jax import lax
from jax.experimental import pallas as pl
from jax.experimental.pallas import tpu as pltpu
from jax.sharding import PartitionSpec as P

F32 = jnp.float32
BF16 = jnp.bfloat16
MESH = pl.DeviceIdType.MESH
ZL = 128


def roll_up(v):
    z = lax.broadcasted_iota(jnp.int32, v.shape, 1) % ZL
    return jnp.where(z == 0, 0.0, pltpu.roll(v, 1, 1))


def roll_down(v):
    z = lax.broadcasted_iota(jnp.int32, v.shape, 1) % ZL
    return jnp.where(z == ZL - 1, 0.0, pltpu.roll(v, v.shape[1] - 1, 1))


def sigmoid(v):
    return 1.0 / (1.0 + jnp.exp(-v))


def slope(v):
    s = sigmoid(v)
    return s * (1.0 + v * (1.0 - s))


def kernel(
    n, cells,
    home, invd, hbias,
    payload, wa, wb, wc, tb, tc, ba, bb, bc, hw,
    pressure, gwa, gwb, gwc, small,
    gath, fwin, x0, h1, z1, h2, z2, z3, h3, im, im2, pv, yb, coef, gsr, g3e, g2e,
    gs_sem, gr_sem, ps_sem, pr_sem, es_sem, er_sem,
):
    gx = lax.axis_index("gx")
    gy = lax.axis_index("gy")
    count = 2 * n
    me = gx * 2 + gy
    other = 1 - gy

    pv[...] = jnp.zeros_like(pv)
    for ext in (g3e, g2e):
        ext[0] = jnp.zeros((64, 1280), BF16)
        ext[3] = jnp.zeros((64, 1280), BF16)
        for x in (1, 2):
            ext[x, :, 0:128] = jnp.zeros((64, 128), BF16)
            ext[x, :, 1152:1280] = jnp.zeros((64, 128), BF16)

    barrier = pltpu.get_barrier_semaphore()
    for k in range(1, count):
        to = lax.rem(me + k, count)
        pl.semaphore_signal(
            barrier, inc=1, device_id={"gx": to // 2, "gy": to % 2}, device_id_type=MESH
        )
    pl.semaphore_wait(barrier, count - 1)

    def gather_copy(k):
        to = lax.rem(me + k, count)
        return pltpu.make_async_remote_copy(
            src_ref=payload,
            dst_ref=gath.at[me],
            send_sem=gs_sem.at[k],
            recv_sem=gr_sem.at[k],
            device_id={"gx": to // 2, "gy": to % 2},
            device_id_type=MESH,
        )

    for k in range(1, count):
        gather_copy(k).start()
    gath[me] = payload[...]
    fwin[...] = jnp.zeros_like(fwin)
    x0[...] = jnp.zeros_like(x0)
    for k in range(1, count):
        gather_copy(k).wait_recv()
    for k in range(1, count):
        gather_copy(k).wait_send()

    for d in range(-2, 3):
        q = gx + d
        valid = jnp.logical_and(q >= 0, q < n)
        geo = jnp.clip(q, 0, n - 1)
        source = jnp.int32(0)
        for s in range(n):
            source = jnp.where(home[s] == q, s, source)
        keep = jnp.where(valid, 1.0, 0.0)
        for w in range(2):
            fields = gath[source * 2 + w].astype(F32)[0:32] * keep
            shape = gath[geo * 2 + w].astype(F32)[32:64] * keep
            both = [fields[0:16], fields[16:32], shape[0:16], shape[16:32]]
            for x in range(2):
                p = 2 * d + x + 3
                if p < 0 or p > 7:
                    continue
                for c in range(4):
                    fwin[c, p, 8 + 8 * w : 16 + 8 * w, :] = both[c][8 * x : 8 * x + 8]

    def spread(p, carry):
        for c in range(3):
            for y in range(14):
                x0[p, c : c + 1, y * 128 : (y + 1) * 128] = fwin[c, p, pl.ds(8 * gy + 5 + y, 1), :]
        return carry

    lax.fori_loop(0, 8, spread, 0)

    def merge_forward(out):
        return roll_up(out[0:64]) + out[64:128] + roll_down(out[128:192])

    def merge_back(out):
        return roll_down(out[0:64]) + out[64:128] + roll_up(out[128:192])

    def patches_a(first, lane, width):
        rows = []
        for a in range(3):
            for b in range(3):
                rows.append(x0[first + a, :, lane + b * 128 : lane + b * 128 + width])
        return jnp.concatenate(rows, axis=0).astype(BF16)

    def fill(dst, src, first, lane, width):
        for a in range(3):
            for b in range(3):
                k = (3 * a + b) * 64
                dst[k : k + 64, 0:width] = src[first + a, :, lane + b * 128 : lane + b * 128 + width]

    def layer_a(x, carry):
        out = jnp.dot(wa[...], patches_a(x, 0, 1536), preferred_element_type=F32)
        z = merge_forward(out) + ba[...]
        z1[x] = z
        h1[x] = (z * sigmoid(z) * x0[x + 1, 2:3, 128 : 128 + 1536]).astype(BF16)
        return carry

    lax.fori_loop(0, 6, layer_a, 0)

    def layer_b(x, carry):
        fill(im, h1, x, 0, 1280)
        out = jnp.dot(wb[...], im[...], preferred_element_type=F32)
        z = merge_forward(out) + bb[...]
        z2[x] = z
        h2[x] = (z * sigmoid(z) * x0[x + 2, 2:3, 256 : 256 + 1280]).astype(BF16)
        return carry

    lax.fori_loop(0, 4, layer_b, 0)

    def layer_c(x, carry):
        fill(im2.at[x], h2, x, 0, 1024)
        out = jnp.dot(wc[...], im2[x], preferred_element_type=F32)
        z = merge_forward(out) + bc[...]
        z3[x] = z
        liquid = x0[x + 3, 2:3, 384 : 384 + 1024]
        h = (z * sigmoid(z) * liquid).astype(BF16).astype(F32)
        h3[x] = h
        score = liquid * (jnp.sum(h * hw[...], axis=0, keepdims=True) + hbias[0])
        for y in range(8):
            pv[0, 1 + x, 8 + y : 9 + y, :] = score[:, y * 128 : (y + 1) * 128]
        return carry

    lax.fori_loop(0, 2, layer_c, 0)
    for x in range(2):
        pressure[x] = pv[0, 1 + x, 8:16, :]

    has_low = gx > 0
    has_high = gx < n - 1
    low = jnp.maximum(gx - 1, 0)
    high = jnp.minimum(gx + 1, n - 1)

    def face_copies(k):
        def make(slot, src, dst, to_x, to_y):
            return pltpu.make_async_remote_copy(
                src_ref=src,
                dst_ref=dst,
                send_sem=ps_sem.at[k, slot],
                recv_sem=pr_sem.at[k, slot],
                device_id={"gx": to_x, "gy": to_y},
                device_id_type=MESH,
            )

        inner = pl.ds(8, 8)
        down = make(0, pv.at[k, 1, inner], pv.at[k, 3, inner], low, gy)
        up = make(1, pv.at[k, 2, inner], pv.at[k, 0, inner], high, gy)
        side = make(2, pv.at[k, pl.ds(1, 2), inner], yb.at[k], gx, other)
        return down, up, side

    def edge_copies(k, ext):
        def make(slot, src, dst, to_x, to_y):
            return pltpu.make_async_remote_copy(
                src_ref=src,
                dst_ref=dst,
                send_sem=es_sem.at[k, slot],
                recv_sem=er_sem.at[k, slot],
                device_id={"gx": to_x, "gy": to_y},
                device_id_type=MESH,
            )

        inner = pl.ds(128, 1024)
        mine = pl.ds(pl.multiple_of(128 * (8 - 7 * gy), 128), 128)
        theirs = pl.ds(pl.multiple_of(1152 * gy, 128), 128)
        down = make(0, ext.at[1, :, inner], ext.at[3, :, inner], low, gy)
        up = make(1, ext.at[2, :, inner], ext.at[0, :, inner], high, gy)
        side = make(2, ext.at[pl.ds(1, 2), :, mine], ext.at[pl.ds(1, 2), :, theirs], gx, other)
        corner_down = make(3, ext.at[1, :, mine], ext.at[3, :, theirs], low, other)
        corner_up = make(4, ext.at[2, :, mine], ext.at[0, :, theirs], high, other)
        return down, up, side, corner_down, corner_up

    def start_all(copies):
        @pl.when(has_low)
        def _():
            for c in copies[0::3]:
                c.start()

        @pl.when(has_high)
        def _():
            for c in copies[1::3]:
                c.start()

        copies[2].start()

    def finish_all(copies):
        @pl.when(has_high)
        def _():
            for c in copies[0::3]:
                c.wait_recv()

        @pl.when(has_low)
        def _():
            for c in copies[1::3]:
                c.wait_recv()

        copies[2].wait_recv()

        @pl.when(has_low)
        def _():
            for c in copies[0::3]:
                c.wait_send()

        @pl.when(has_high)
        def _():
            for c in copies[1::3]:
                c.wait_send()

        copies[2].wait_send()

    start_all(face_copies(0))

    def geometry(p):
        window = pl.ds(pl.multiple_of(8 * gy, 8), 24)
        liquid = fwin[2, p, window, :]
        kind = fwin[3, p, window, :]
        scale = jnp.zeros_like(kind)
        for c in range(4):
            scale = scale + jnp.where(kind == c, invd[c], 0.0)
        return scale * liquid, liquid

    geo = [geometry(p) for p in range(2, 6)]
    for x in range(2):
        scaled, liquid = geo[x + 1]
        s0, l0 = scaled[8:16], liquid[8:16]
        nears = [
            tuple(v[8:16] for v in geo[x + 2]),
            tuple(v[8:16] for v in geo[x]),
            (scaled[9:17], liquid[9:17]),
            (scaled[7:15], liquid[7:15]),
            (roll_down(s0), roll_down(l0)),
            (roll_up(s0), roll_up(l0)),
        ]
        for j, (ns, nl) in enumerate(nears):
            coef[x, j] = 0.5 * (s0 * nl + ns * l0)

    def operate(k, x):
        v = pv[k, 1 + x, 8:16, :]
        nears = [
            pv[k, 2 + x, 8:16, :],
            pv[k, x, 8:16, :],
            pv[k, 1 + x, 9:17, :],
            pv[k, 1 + x, 7:15, :],
            pltpu.roll(v, ZL - 1, 1),
            pltpu.roll(v, 1, 1),
        ]
        total = jnp.zeros_like(v)
        for j, near in enumerate(nears):
            total = total + coef[x, j] * (near - v)
        return total

    def sides(k):
        for x in range(2):
            pv[k, 1 + x, 7:8, :] = yb[k, x, 7:8, :]
            pv[k, 1 + x, 16:17, :] = yb[k, x, 0:1, :]

    here = pl.ds(pl.multiple_of(8 * gy + 8, 8), 8)
    finish_all(face_copies(0))
    sides(0)
    squares = jnp.zeros((8, 128), F32)
    for x in range(2):
        residual = operate(0, x) - fwin[2, 3 + x, here, :] * fwin[1, 3 + x, here, :]
        squares = squares + residual * residual
        pv[1, 1 + x, 8:16, :] = 2.0 * residual / cells
    start_all(face_copies(1))
    loss = jnp.sum(jnp.sum(squares, axis=1, keepdims=True), axis=0, keepdims=True) / cells
    finish_all(face_copies(1))
    sides(1)
    for x in range(2):
        score = fwin[2, 3 + x, here, :] * operate(1, x)
        for y in range(8):
            gsr[x, :, y * 128 : (y + 1) * 128] = score[y : y + 1, :]

    def sum_cells(v):
        return jnp.sum(v, axis=1, keepdims=True)

    def three(g):
        gf = g.astype(F32)
        return jnp.concatenate([roll_down(gf), gf, roll_up(gf)], axis=0).astype(BF16)

    def wgrad(g, rows):
        return lax.dot_general(
            three(g), rows, (((1,), (1,)), ((), ())), preferred_element_type=F32
        )

    inner = slice(128, 1152)
    grad_head = jnp.zeros((64, 1), F32)
    grad_bc = jnp.zeros((64, 1), F32)
    for x in range(2):
        gs = gsr[x]
        liquid = x0[x + 3, 2:3, 384 : 384 + 1024]
        g = (gs * hw[...] * liquid * slope(z3[x])).astype(BF16)
        g3e[1 + x, :, inner] = g
    start_all(edge_copies(0, g3e))
    for x in range(2):
        grad_head = grad_head + sum_cells(gsr[x] * h3[x])
        g = g3e[1 + x, :, inner]
        grad_bc = grad_bc + sum_cells(g.astype(F32))
        part = wgrad(g, im2[x])
        gwc[...] = part if x == 0 else gwc[...] + part
    finish_all(edge_copies(0, g3e))

    def fill_back(dst, src, x):
        for a in range(3):
            for b in range(3):
                k = (3 * a + b) * 64
                dst[k : k + 64, :] = src[x + 2 - a, :, (2 - b) * 128 : (2 - b) * 128 + 1024]

    grad_bb = jnp.zeros((64, 1), F32)
    for x in range(2):
        fill_back(im2.at[x], g3e, x)
        out = jnp.dot(tc[...], im2[x], preferred_element_type=F32)
        liquid = x0[x + 3, 2:3, 384 : 384 + 1024]
        g = merge_back(out) * liquid * slope(z2[x + 1, :, 128 : 128 + 1024])
        g2e[1 + x, :, inner] = g.astype(BF16)
    start_all(edge_copies(1, g2e))
    for x in range(2):
        fill(im2.at[x], h1, x + 1, 128, 1024)
        g = g2e[1 + x, :, inner]
        grad_bb = grad_bb + sum_cells(g.astype(F32))
        part = wgrad(g, im2[x])
        gwb[...] = part if x == 0 else gwb[...] + part
    finish_all(edge_copies(1, g2e))

    grad_ba = jnp.zeros((64, 1), F32)
    for x in range(2):
        fill_back(im2.at[x], g2e, x)
        out = jnp.dot(tb[...], im2[x], preferred_element_type=F32)
        liquid = x0[x + 3, 2:3, 384 : 384 + 1024]
        g = (merge_back(out) * liquid * slope(z1[x + 2, :, 256 : 256 + 1024])).astype(BF16)
        grad_ba = grad_ba + sum_cells(g.astype(F32))
        part = wgrad(g, patches_a(x + 2, 256, 1024))
        gwa[...] = part if x == 0 else gwa[...] + part

    lane = lax.broadcasted_iota(jnp.int32, (64, 128), 1)
    packed = jnp.where(lane == 0, grad_ba, 0.0)
    packed = jnp.where(lane == 1, grad_bb, packed)
    packed = jnp.where(lane == 2, grad_bc, packed)
    packed = jnp.where(lane == 3, grad_head, packed)
    packed = jnp.where(lane == 4, loss, packed)
    small[...] = packed


def on_device(
    loaded_fields, brick_home, liquid_mask, density_class, inverse_density,
    conv_a, bias_a, conv_b, bias_b, conv_c, bias_c, head_weight, head_bias,
):
    n = lax.axis_size("gx")
    count = 2 * n
    payload = jnp.concatenate(
        [
            loaded_fields.reshape(32, 128),
            liquid_mask.astype(BF16).reshape(16, 128),
            density_class.astype(BF16).reshape(16, 128),
        ],
        axis=0,
    )

    def forward(w):
        w = w.reshape(3, 3, 3, 64, w.shape[-1]).transpose(2, 3, 0, 1, 4)
        return w.reshape(192, -1)

    def backward(w):
        return w.reshape(3, 3, 3, 64, 64).transpose(2, 4, 0, 1, 3).reshape(192, 576)

    wa = forward(jnp.pad(conv_a, ((0, 0), (0, 0), (0, 5))))
    vmem = pl.BlockSpec(memory_space=pltpu.VMEM)
    smem = pl.BlockSpec(memory_space=pltpu.SMEM)
    pressure, gwa, gwb, gwc, small = pl.pallas_call(
        functools.partial(kernel, n, float(2 * n * 16 * 128)),
        out_shape=(
            jax.ShapeDtypeStruct((2, 8, 128), F32),
            jax.ShapeDtypeStruct((192, 72), F32),
            jax.ShapeDtypeStruct((192, 576), F32),
            jax.ShapeDtypeStruct((192, 576), F32),
            jax.ShapeDtypeStruct((64, 128), F32),
        ),
        in_specs=[smem] * 3 + [vmem] * 10,
        out_specs=(vmem,) * 5,
        scratch_shapes=[
            pltpu.VMEM((count, 64, 128), BF16),
            pltpu.VMEM((4, 8, 32, 128), F32),
            pltpu.VMEM((8, 8, 14 * 128), F32),
            pltpu.VMEM((6, 64, 1536), BF16),
            pltpu.VMEM((6, 64, 1536), F32),
            pltpu.VMEM((4, 64, 1280), BF16),
            pltpu.VMEM((4, 64, 1280), F32),
            pltpu.VMEM((2, 64, 1024), F32),
            pltpu.VMEM((2, 64, 1024), F32),
            pltpu.VMEM((576, 1280), BF16),
            pltpu.VMEM((2, 576, 1024), BF16),
            pltpu.VMEM((2, 4, 24, 128), F32),
            pltpu.VMEM((2, 2, 8, 128), F32),
            pltpu.VMEM((2, 6, 8, 128), F32),
            pltpu.VMEM((2, 1, 1024), F32),
            pltpu.VMEM((4, 64, 1280), BF16),
            pltpu.VMEM((4, 64, 1280), BF16),
            pltpu.SemaphoreType.DMA((count,)),
            pltpu.SemaphoreType.DMA((count,)),
            pltpu.SemaphoreType.DMA((2, 3)),
            pltpu.SemaphoreType.DMA((2, 3)),
            pltpu.SemaphoreType.DMA((2, 5)),
            pltpu.SemaphoreType.DMA((2, 5)),
        ],
        compiler_params=pltpu.CompilerParams(
            collective_id=0, has_side_effects=True, vmem_limit_bytes=48 * 1024 * 1024
        ),
    )(
        brick_home, inverse_density, head_bias,
        payload, wa, forward(conv_b), forward(conv_c), backward(conv_b), backward(conv_c),
        bias_a.reshape(64, 1), bias_b.reshape(64, 1), bias_c.reshape(64, 1),
        head_weight.astype(F32).reshape(64, 1),
    )
    gwa, gwb, gwc, small = lax.psum((gwa, gwb, gwc, small), ("gx", "gy"))

    def taps(g, width):
        g = g.reshape(3, 64, 3, 3, -1)[..., :width].transpose(2, 3, 0, 1, 4)
        return g.reshape(27, 64, width)

    return (
        pressure, small[0, 4:5],
        taps(gwa, 3), small[:, 0], taps(gwb, 64), small[:, 1], taps(gwc, 64), small[:, 2],
        small[:, 3],
    )


def solution(mesh):
    placed = (
        P(None, ("grp", "gx"), "gy", None),
        P("grp"),
        P(("grp", "gx"), "gy", None),
        P(("grp", "gx"), "gy", None),
    ) + (P(),) * 9
    return jax.shard_map(
        on_device,
        mesh=mesh,
        in_specs=placed,
        out_specs=(
            P(("grp", "gx"), "gy", None),
            P("grp"),
            P("grp", None, None),
            P("grp"),
            P("grp", None, None),
            P("grp"),
            P("grp", None, None),
            P("grp"),
            P("grp"),
        ),
        check_vma=False,
    )
```

```python
import functools

import jax
import jax.numpy as jnp
from jax import lax
from jax.experimental import pallas as pl
from jax.experimental.pallas import tpu as pltpu
from jax.sharding import PartitionSpec as P

F32 = jnp.float32
BF16 = jnp.bfloat16
MESH = pl.DeviceIdType.MESH
ZL = 128


def roll_up(v):
    z = lax.broadcasted_iota(jnp.int32, v.shape, 1) % ZL
    return jnp.where(z == 0, 0.0, pltpu.roll(v, 1, 1))


def roll_down(v):
    z = lax.broadcasted_iota(jnp.int32, v.shape, 1) % ZL
    return jnp.where(z == ZL - 1, 0.0, pltpu.roll(v, v.shape[1] - 1, 1))


def sigmoid(v):
    return 1.0 / (1.0 + jnp.exp(-v))


def slope(v):
    s = sigmoid(v)
    return s * (1.0 + v * (1.0 - s))


def kernel(
    n, cells, chunks,
    home, invd, hbias,
    payload, wa, cb, cc, ba, bb, bc, hw,
    pressure, out_a, out_b, out_c, small,
    gath, fwin, x0, h1, z1, h2, z2, z3, h3, im, im2, pv, yb, coef, gsr, g3e, g2e,
    wb, wc, tb, tc, gwa, gwb, gwc, raw_c, raw_b, near_c, near_b, sum_c, sum_b, land_c, land_b, full_c, full_b, tiny,
    gs_sem, gr_sem, ps_sem, pr_sem, es_sem, er_sem, ws_sem, wr_sem, ts_sem, tr_sem,
):
    gx = lax.axis_index("gx")
    gy = lax.axis_index("gy")
    count = 2 * n
    me = gx * 2 + gy
    other = 1 - gy

    pv[...] = jnp.zeros_like(pv)
    raw_c[...] = jnp.zeros_like(raw_c)
    raw_b[...] = jnp.zeros_like(raw_b)
    for ext in (g3e, g2e):
        ext[0] = jnp.zeros((64, 1280), BF16)
        ext[3] = jnp.zeros((64, 1280), BF16)
        for x in (1, 2):
            ext[x, :, 0:128] = jnp.zeros((64, 128), BF16)
            ext[x, :, 1152:1280] = jnp.zeros((64, 128), BF16)

    barrier = pltpu.get_barrier_semaphore()
    for k in range(1, count):
        to = lax.rem(me + k, count)
        pl.semaphore_signal(
            barrier, inc=1, device_id={"gx": to // 2, "gy": to % 2}, device_id_type=MESH
        )
    pl.semaphore_wait(barrier, count - 1)

    def gather_copy(k):
        to = lax.rem(me + k, count)
        return pltpu.make_async_remote_copy(
            src_ref=payload,
            dst_ref=gath.at[me],
            send_sem=gs_sem.at[k],
            recv_sem=gr_sem.at[k],
            device_id={"gx": to // 2, "gy": to % 2},
            device_id_type=MESH,
        )

    for k in range(1, count):
        gather_copy(k).start()
    gath[me] = payload[...]
    fwin[...] = jnp.zeros_like(fwin)
    x0[...] = jnp.zeros_like(x0)
    for wide, conv in ((wb, cb), (wc, cc)):
        for t in range(27):
            k, e = t // 3 * 64, t % 3 * 64
            wide[e : e + 64, k : k + 64] = conv[t]
    for k in range(1, count):
        gather_copy(k).wait_recv()
    for k in range(1, count):
        gather_copy(k).wait_send()

    for d in range(-2, 3):
        q = gx + d
        valid = jnp.logical_and(q >= 0, q < n)
        geo = jnp.clip(q, 0, n - 1)
        source = jnp.int32(0)
        for s in range(n):
            source = jnp.where(home[s] == q, s, source)
        keep = jnp.where(valid, 1.0, 0.0)
        for w in range(2):
            fields = gath[source * 2 + w].astype(F32)[0:32] * keep
            shape = gath[geo * 2 + w].astype(F32)[32:64] * keep
            both = [fields[0:16], fields[16:32], shape[0:16], shape[16:32]]
            for x in range(2):
                p = 2 * d + x + 3
                if p < 0 or p > 7:
                    continue
                for c in range(4):
                    fwin[c, p, 8 + 8 * w : 16 + 8 * w, :] = both[c][8 * x : 8 * x + 8]

    def spread(p, carry):
        for c in range(3):
            for y in range(14):
                x0[p, c : c + 1, y * 128 : (y + 1) * 128] = fwin[c, p, pl.ds(8 * gy + 5 + y, 1), :]
        return carry

    lax.fori_loop(0, 8, spread, 0)

    def merge_forward(out):
        return roll_up(out[0:64]) + out[64:128] + roll_down(out[128:192])

    def merge_back(out):
        return roll_down(out[0:64]) + out[64:128] + roll_up(out[128:192])

    def patches_a(first, lane, width):
        rows = []
        for a in range(3):
            for b in range(3):
                rows.append(x0[first + a, :, lane + b * 128 : lane + b * 128 + width])
        return jnp.concatenate(rows, axis=0).astype(BF16)

    def fill(dst, src, first, lane, width):
        for a in range(3):
            for b in range(3):
                k = (3 * a + b) * 64
                dst[k : k + 64, 0:width] = src[first + a, :, lane + b * 128 : lane + b * 128 + width]

    def layer_a(x, carry):
        out = jnp.dot(wa[...], patches_a(x, 0, 1536), preferred_element_type=F32)
        z = merge_forward(out) + ba[...]
        z1[x] = z
        h1[x] = (z * sigmoid(z) * x0[x + 1, 2:3, 128 : 128 + 1536]).astype(BF16)
        return carry

    lax.fori_loop(0, 6, layer_a, 0)

    def layer_b(x, carry):
        fill(im, h1, x, 0, 1280)
        out = jnp.dot(wb[...], im[...], preferred_element_type=F32)
        z = merge_forward(out) + bb[...]
        z2[x] = z
        h2[x] = (z * sigmoid(z) * x0[x + 2, 2:3, 256 : 256 + 1280]).astype(BF16)
        return carry

    lax.fori_loop(0, 4, layer_b, 0)

    def layer_c(x, carry):
        fill(im2.at[x], h2, x, 0, 1024)
        out = jnp.dot(wc[...], im2[x], preferred_element_type=F32)
        z = merge_forward(out) + bc[...]
        z3[x] = z
        liquid = x0[x + 3, 2:3, 384 : 384 + 1024]
        h = (z * sigmoid(z) * liquid).astype(BF16).astype(F32)
        h3[x] = h
        score = liquid * (jnp.sum(h * hw[...], axis=0, keepdims=True) + hbias[0])
        for y in range(8):
            pv[0, 1 + x, 8 + y : 9 + y, :] = score[:, y * 128 : (y + 1) * 128]
        return carry

    lax.fori_loop(0, 2, layer_c, 0)
    for x in range(2):
        pressure[x] = pv[0, 1 + x, 8:16, :]

    has_low = gx > 0
    has_high = gx < n - 1
    low = jnp.maximum(gx - 1, 0)
    high = jnp.minimum(gx + 1, n - 1)

    def face_copies(k):
        def make(slot, src, dst, to_x, to_y):
            return pltpu.make_async_remote_copy(
                src_ref=src,
                dst_ref=dst,
                send_sem=ps_sem.at[k, slot],
                recv_sem=pr_sem.at[k, slot],
                device_id={"gx": to_x, "gy": to_y},
                device_id_type=MESH,
            )

        inner = pl.ds(8, 8)
        down = make(0, pv.at[k, 1, inner], pv.at[k, 3, inner], low, gy)
        up = make(1, pv.at[k, 2, inner], pv.at[k, 0, inner], high, gy)
        side = make(2, pv.at[k, pl.ds(1, 2), inner], yb.at[k], gx, other)
        return down, up, side

    def edge_copies(k, ext):
        def make(slot, src, dst, to_x, to_y):
            return pltpu.make_async_remote_copy(
                src_ref=src,
                dst_ref=dst,
                send_sem=es_sem.at[k, slot],
                recv_sem=er_sem.at[k, slot],
                device_id={"gx": to_x, "gy": to_y},
                device_id_type=MESH,
            )

        inner = pl.ds(128, 1024)
        mine = pl.ds(pl.multiple_of(128 * (8 - 7 * gy), 128), 128)
        theirs = pl.ds(pl.multiple_of(1152 * gy, 128), 128)
        down = make(0, ext.at[1, :, inner], ext.at[3, :, inner], low, gy)
        up = make(1, ext.at[2, :, inner], ext.at[0, :, inner], high, gy)
        side = make(2, ext.at[pl.ds(1, 2), :, mine], ext.at[pl.ds(1, 2), :, theirs], gx, other)
        corner_down = make(3, ext.at[1, :, mine], ext.at[3, :, theirs], low, other)
        corner_up = make(4, ext.at[2, :, mine], ext.at[0, :, theirs], high, other)
        return down, up, side, corner_down, corner_up

    def start_all(copies):
        @pl.when(has_low)
        def _():
            for c in copies[0::3]:
                c.start()

        @pl.when(has_high)
        def _():
            for c in copies[1::3]:
                c.start()

        copies[2].start()

    def finish_all(copies):
        @pl.when(has_high)
        def _():
            for c in copies[0::3]:
                c.wait_recv()

        @pl.when(has_low)
        def _():
            for c in copies[1::3]:
                c.wait_recv()

        copies[2].wait_recv()

        @pl.when(has_low)
        def _():
            for c in copies[0::3]:
                c.wait_send()

        @pl.when(has_high)
        def _():
            for c in copies[1::3]:
                c.wait_send()

        copies[2].wait_send()

    start_all(face_copies(0))
    for x in range(2):
        z3[x] = x0[x + 3, 2:3, 384 : 384 + 1024] * slope(z3[x])
    for t in range(27):
        k, e = t // 3 * 64, t % 3 * 64
        tc[e : e + 64, k : k + 64] = cc[t].astype(F32).T.astype(BF16)

    def geometry(p):
        window = pl.ds(pl.multiple_of(8 * gy, 8), 24)
        liquid = fwin[2, p, window, :]
        kind = fwin[3, p, window, :]
        scale = jnp.zeros_like(kind)
        for c in range(4):
            scale = scale + jnp.where(kind == c, invd[c], 0.0)
        return scale * liquid, liquid

    geo = [geometry(p) for p in range(2, 6)]
    for x in range(2):
        scaled, liquid = geo[x + 1]
        s0, l0 = scaled[8:16], liquid[8:16]
        nears = [
            tuple(v[8:16] for v in geo[x + 2]),
            tuple(v[8:16] for v in geo[x]),
            (scaled[9:17], liquid[9:17]),
            (scaled[7:15], liquid[7:15]),
            (roll_down(s0), roll_down(l0)),
            (roll_up(s0), roll_up(l0)),
        ]
        for j, (ns, nl) in enumerate(nears):
            coef[x, j] = 0.5 * (s0 * nl + ns * l0)

    def operate(k, x):
        v = pv[k, 1 + x, 8:16, :]
        nears = [
            pv[k, 2 + x, 8:16, :],
            pv[k, x, 8:16, :],
            pv[k, 1 + x, 9:17, :],
            pv[k, 1 + x, 7:15, :],
            pltpu.roll(v, ZL - 1, 1),
            pltpu.roll(v, 1, 1),
        ]
        total = jnp.zeros_like(v)
        for j, near in enumerate(nears):
            total = total + coef[x, j] * (near - v)
        return total

    def sides(k):
        for x in range(2):
            pv[k, 1 + x, 7:8, :] = yb[k, x, 7:8, :]
            pv[k, 1 + x, 16:17, :] = yb[k, x, 0:1, :]

    here = pl.ds(pl.multiple_of(8 * gy + 8, 8), 8)
    finish_all(face_copies(0))
    sides(0)
    squares = jnp.zeros((8, 128), F32)
    for x in range(2):
        residual = operate(0, x) - fwin[2, 3 + x, here, :] * fwin[1, 3 + x, here, :]
        squares = squares + residual * residual
        pv[1, 1 + x, 8:16, :] = 2.0 * residual / cells
    start_all(face_copies(1))
    for x in range(2):
        liquid = x0[x + 3, 2:3, 384 : 384 + 1024]
        z2[x + 1, :, 128 : 128 + 1024] = liquid * slope(z2[x + 1, :, 128 : 128 + 1024])
        z1[x + 2, :, 256 : 256 + 1024] = liquid * slope(z1[x + 2, :, 256 : 256 + 1024])
    for t in range(27):
        k, e = t // 3 * 64, t % 3 * 64
        tb[e : e + 64, k : k + 64] = cb[t].astype(F32).T.astype(BF16)
    loss = jnp.sum(jnp.sum(squares, axis=1, keepdims=True), axis=0, keepdims=True) / cells
    finish_all(face_copies(1))
    sides(1)
    for x in range(2):
        score = fwin[2, 3 + x, here, :] * operate(1, x)
        for y in range(8):
            gsr[x, :, y * 128 : (y + 1) * 128] = score[y : y + 1, :]

    def sum_cells(v):
        return jnp.sum(v, axis=1, keepdims=True)

    def three(g):
        gf = g.astype(F32)
        return jnp.concatenate([roll_down(gf), gf, roll_up(gf)], axis=0).astype(BF16)

    def wgrad(g, rows):
        return lax.dot_general(
            three(g), rows, (((1,), (1,)), ((), ())), preferred_element_type=F32
        )

    inner = slice(128, 1152)
    raws, nears, sums = (raw_c, raw_b), (near_c, near_b), (sum_c, sum_b)
    lands, fulls = (land_c, land_b), (full_c, full_b)

    def weight_copy(i, slot, src, dst, to_x, to_y):
        return pltpu.make_async_remote_copy(
            src_ref=src,
            dst_ref=dst,
            send_sem=ws_sem.at[i, slot],
            recv_sem=wr_sem.at[i, slot],
            device_id={"gx": to_x, "gy": to_y},
            device_id_type=MESH,
        )

    def rows_at(start, length):
        return pl.ds(pl.multiple_of(start, 16), length)

    def pair_copy(i):
        half = n * chunks[i]
        return weight_copy(i, 0, raws[i].at[rows_at(other * half, half)], nears[i], gx, other)

    def scatter_copies(i):
        c = chunks[i]
        made = []
        for k in range(1, n):
            to = lax.rem(gx + k, n)
            made.append(
                weight_copy(i, 2 + k, sums[i].at[rows_at(to * c, c)], lands[i].at[k], to, gy)
            )
        return made

    def gather_copies(i):
        c = chunks[i]
        place = fulls[i].at[rows_at((gy * n + gx) * c, c)]
        return [
            weight_copy(i, 2 + n + k, place, place, lax.rem(gx + k, n), gy) for k in range(1, n)
        ]

    def last_copy(i):
        half = n * chunks[i]
        place = fulls[i].at[rows_at(gy * half, half)]
        return weight_copy(i, 1, place, place, gx, other)

    def wait_copies(copies):
        for c in copies:
            c.wait_recv()
        for c in copies:
            c.wait_send()

    def start_copies(copies):
        for c in copies:
            c.start()

    def pair_to_scatter(i):
        half = n * chunks[i]
        wait_copies([pair_copy(i)])
        mine = raws[i][rows_at(gy * half, half), :].astype(F32)
        sums[i][...] = (mine + nears[i][...].astype(F32)).astype(BF16)
        start_copies(scatter_copies(i))

    def scatter_to_gather(i):
        c = chunks[i]
        wait_copies(scatter_copies(i))
        total = sums[i][rows_at(gx * c, c), :].astype(F32)
        for k in range(1, n):
            total = total + lands[i][k].astype(F32)
        fulls[i][rows_at((gy * n + gx) * c, c), :] = total.astype(BF16)
        start_copies(gather_copies(i))

    def gather_to_last(i):
        wait_copies(gather_copies(i))
        last_copy(i).start()

    def pack(raw, value, first):
        for j in range(-(-value.shape[1] // 128)):
            part = value[:, j * 128 : (j + 1) * 128]
            if part.shape[1] < 128:
                fill_in = jnp.zeros((192, 128 - part.shape[1]), F32)
                part = jnp.concatenate([part, fill_in], axis=1)
            raw[(first + j) * 192 : (first + j + 1) * 192, :] = part.astype(BF16)

    def unpack(out, full, first, step, width):
        for a in range(9):
            tile, lane = (a * step) // 128, (a * step) % 128
            for e in range(3):
                row = (first + tile) * 192 + e * 64
                part = full[row : row + 64, :].astype(F32)
                out[3 * a + e] = part[:, lane : lane + width]

    grad_head = jnp.zeros((64, 1), F32)
    grad_bc = jnp.zeros((64, 1), F32)
    for x in range(2):
        gs = gsr[x]
        g = (gs * hw[...] * z3[x]).astype(BF16)
        g3e[1 + x, :, inner] = g
    start_all(edge_copies(0, g3e))
    for x in range(2):
        grad_head = grad_head + sum_cells(gsr[x] * h3[x])
        g = g3e[1 + x, :, inner]
        grad_bc = grad_bc + sum_cells(g.astype(F32))
        part = wgrad(g, im2[x])
        gwc[...] = part if x == 0 else gwc[...] + part
    pack(raw_c, gwc[...], 0)
    pair_copy(0).start()
    finish_all(edge_copies(0, g3e))

    def fill_back(dst, src, x):
        for a in range(3):
            for b in range(3):
                k = (3 * a + b) * 64
                dst[k : k + 64, :] = src[x + 2 - a, :, (2 - b) * 128 : (2 - b) * 128 + 1024]

    grad_bb = jnp.zeros((64, 1), F32)
    for x in range(2):
        fill_back(im2.at[x], g3e, x)
        out = jnp.dot(tc[...], im2[x], preferred_element_type=F32)
        g = merge_back(out) * z2[x + 1, :, 128 : 128 + 1024]
        g2e[1 + x, :, inner] = g.astype(BF16)
    start_all(edge_copies(1, g2e))
    pair_to_scatter(0)
    for x in range(2):
        fill(im2.at[x], h1, x + 1, 128, 1024)
        g = g2e[1 + x, :, inner]
        grad_bb = grad_bb + sum_cells(g.astype(F32))
        part = wgrad(g, im2[x])
        gwb[...] = part if x == 0 else gwb[...] + part
    finish_all(edge_copies(1, g2e))

    grad_ba = jnp.zeros((64, 1), F32)
    for x in range(2):
        fill_back(im2.at[x], g2e, x)
        out = jnp.dot(tb[...], im2[x], preferred_element_type=F32)
        g = (merge_back(out) * z1[x + 2, :, 256 : 256 + 1024]).astype(BF16)
        grad_ba = grad_ba + sum_cells(g.astype(F32))
        part = wgrad(g, patches_a(x + 2, 256, 1024))
        gwa[...] = part if x == 0 else gwa[...] + part

    pack(raw_b, gwb[...], 0)
    pack(raw_b, gwa[...], 5)
    pair_copy(1).start()

    lane = lax.broadcasted_iota(jnp.int32, (64, 128), 1)
    packed = jnp.where(lane == 0, grad_ba, 0.0)
    packed = jnp.where(lane == 1, grad_bb, packed)
    packed = jnp.where(lane == 2, grad_bc, packed)
    packed = jnp.where(lane == 3, grad_head, packed)
    packed = jnp.where(lane == 4, loss, packed)
    turned = packed.T[0:8]
    tiny[me] = jnp.concatenate([turned, turned], axis=1)

    def tiny_copy(k):
        to = lax.rem(me + k, count)
        return pltpu.make_async_remote_copy(
            src_ref=tiny.at[me],
            dst_ref=tiny.at[me],
            send_sem=ts_sem.at[k],
            recv_sem=tr_sem.at[k],
            device_id={"gx": to // 2, "gy": to % 2},
            device_id_type=MESH,
        )

    tiny_copies = [tiny_copy(k) for k in range(1, count)]
    start_copies(tiny_copies)
    scatter_to_gather(0)
    pair_to_scatter(1)
    gather_to_last(0)
    scatter_to_gather(1)
    wait_copies(tiny_copies)
    total = tiny[0]
    for k in range(1, count):
        total = total + tiny[k]
    small[...] = total
    wait_copies([last_copy(0)])
    unpack(out_c, full_c, 0, 64, 64)
    gather_to_last(1)
    wait_copies([last_copy(1)])
    unpack(out_b, full_b, 0, 64, 64)
    unpack(out_a, full_b, 5, 8, 3)


def on_device(
    loaded_fields, brick_home, liquid_mask, density_class, inverse_density,
    conv_a, bias_a, conv_b, bias_b, conv_c, bias_c, head_weight, head_bias,
):
    n = lax.axis_size("gx")
    count = 2 * n
    payload = jnp.concatenate(
        [
            loaded_fields.reshape(32, 128),
            liquid_mask.astype(BF16).reshape(16, 128),
            density_class.astype(BF16).reshape(16, 128),
        ],
        axis=0,
    )

    def forward(w):
        w = w.reshape(3, 3, 3, 64, w.shape[-1]).transpose(2, 3, 0, 1, 4)
        return w.reshape(192, -1)

    wa = forward(jnp.pad(conv_a, ((0, 0), (0, 0), (0, 5))))
    vmem = pl.BlockSpec(memory_space=pltpu.VMEM)
    smem = pl.BlockSpec(memory_space=pltpu.SMEM)
    chunks = tuple(-(-rows // (count * 16)) * 16 for rows in (960, 1152))
    halves = tuple(n * c for c in chunks)
    pressure, gwa, gwb, gwc, small = pl.pallas_call(
        functools.partial(kernel, n, float(2 * n * 16 * 128), chunks),
        out_shape=(
            jax.ShapeDtypeStruct((2, 8, 128), F32),
            jax.ShapeDtypeStruct((27, 64, 3), F32),
            jax.ShapeDtypeStruct((27, 64, 64), F32),
            jax.ShapeDtypeStruct((27, 64, 64), F32),
            jax.ShapeDtypeStruct((8, 128), F32),
        ),
        in_specs=[smem] * 3 + [vmem] * 8,
        out_specs=(vmem,) * 5,
        scratch_shapes=[
            pltpu.VMEM((count, 64, 128), BF16),
            pltpu.VMEM((4, 8, 32, 128), F32),
            pltpu.VMEM((8, 8, 14 * 128), F32),
            pltpu.VMEM((6, 64, 1536), BF16),
            pltpu.VMEM((6, 64, 1536), F32),
            pltpu.VMEM((4, 64, 1280), BF16),
            pltpu.VMEM((4, 64, 1280), F32),
            pltpu.VMEM((2, 64, 1024), F32),
            pltpu.VMEM((2, 64, 1024), F32),
            pltpu.VMEM((576, 1280), BF16),
            pltpu.VMEM((2, 576, 1024), BF16),
            pltpu.VMEM((2, 4, 24, 128), F32),
            pltpu.VMEM((2, 2, 8, 128), F32),
            pltpu.VMEM((2, 6, 8, 128), F32),
            pltpu.VMEM((2, 1, 1024), F32),
            pltpu.VMEM((4, 64, 1280), BF16),
            pltpu.VMEM((4, 64, 1280), BF16),
            pltpu.VMEM((192, 576), BF16),
            pltpu.VMEM((192, 576), BF16),
            pltpu.VMEM((192, 576), BF16),
            pltpu.VMEM((192, 576), BF16),
            pltpu.VMEM((192, 72), F32),
            pltpu.VMEM((192, 576), F32),
            pltpu.VMEM((192, 576), F32),
            pltpu.VMEM((2 * halves[0], 128), BF16),
            pltpu.VMEM((2 * halves[1], 128), BF16),
            pltpu.VMEM((halves[0], 128), BF16),
            pltpu.VMEM((halves[1], 128), BF16),
            pltpu.VMEM((halves[0], 128), BF16),
            pltpu.VMEM((halves[1], 128), BF16),
            pltpu.VMEM((n, chunks[0], 128), BF16),
            pltpu.VMEM((n, chunks[1], 128), BF16),
            pltpu.VMEM((2 * halves[0], 128), BF16),
            pltpu.VMEM((2 * halves[1], 128), BF16),
            pltpu.VMEM((count, 8, 128), F32),
            pltpu.SemaphoreType.DMA((count,)),
            pltpu.SemaphoreType.DMA((count,)),
            pltpu.SemaphoreType.DMA((2, 3)),
            pltpu.SemaphoreType.DMA((2, 3)),
            pltpu.SemaphoreType.DMA((2, 5)),
            pltpu.SemaphoreType.DMA((2, 5)),
            pltpu.SemaphoreType.DMA((2, 2 + 2 * n)),
            pltpu.SemaphoreType.DMA((2, 2 + 2 * n)),
            pltpu.SemaphoreType.DMA((count,)),
            pltpu.SemaphoreType.DMA((count,)),
        ],
        compiler_params=pltpu.CompilerParams(
            collective_id=0, has_side_effects=True, vmem_limit_bytes=48 * 1024 * 1024
        ),
    )(
        brick_home, inverse_density, head_bias,
        payload, wa, conv_b, conv_c,
        bias_a.reshape(64, 1), bias_b.reshape(64, 1), bias_c.reshape(64, 1),
        head_weight.astype(F32).reshape(64, 1),
    )
    return (
        pressure, small[4, 0:1],
        gwa, small[0, 0:64], gwb, small[1, 0:64], gwc, small[2, 0:64],
        small[3, 0:64],
    )


def solution(mesh):
    placed = (
        P(None, ("grp", "gx"), "gy", None),
        P("grp"),
        P(("grp", "gx"), "gy", None),
        P(("grp", "gx"), "gy", None),
    ) + (P(),) * 9
    return jax.shard_map(
        on_device,
        mesh=mesh,
        in_specs=placed,
        out_specs=(
            P(("grp", "gx"), "gy", None),
            P("grp"),
            P("grp", None, None),
            P("grp"),
            P("grp", None, None),
            P("grp"),
            P("grp", None, None),
            P("grp"),
            P("grp"),
        ),
        check_vma=False,
    )
```
